32 devices in a mesh: blk: 8 (over z, core), dp: 4 (over y, x).
Axes of the slice: x: 2, y: 2, z: 4, core: 2. Of those that a mesh axis runs over, the one named last changes fastest.
Arguments:
- queries: bfloat16 [64, 64, 1024], P(('dp', 'blk')), parts along dimension 0, may hold values from -8 to 8, as said below
- keys: bfloat16 [64, 64, 1024], P(('dp', 'blk')), parts along dimension 0, may hold values from -8 to 8, as said below
- values: bfloat16 [64, 64, 1024], P(('dp', 'blk')), parts along dimension 0, may hold values from -6 to 6
Outputs:
- attended: bfloat16 [64, 64, 1024], P(('dp', 'blk')), parts along dimension 0
The draws below stay inside these ranges and needn't reach their ends.
There are 4 independent parts, one for each index of `dp`. The reference program is written for one: setup_inputs(seed, part) draws one part's arguments, and reference() takes and returns one part's arrays. A program takes and returns all parts, laid end to end along the dimension named above; each array names one. Nothing has to cross between parts.
Inputs may be any that keep to these rules, and one draw needn't show every extreme that they name: `queries`: queries of one pixel block. `keys`: keys of one pixel block.
All inputs are finite; a program needn't handle non-finite values.
Results may differ from the reference program's by a relative error of at most 0.0046.
Values may be sent and summed in bfloat16 or wider, within the bound.
A program may use at most 128 MiB of HBM per device.

```python
import jax
import jax.numpy as jnp
from jax import lax

PATCHES = 64
HEADS = 8
HDIM = 128
BANDS = 16
WIDTH = 1024


def drawn_pair(key):
    shape = (BANDS, PATCHES, HEADS * HDIM)
    query_key = jax.random.fold_in(key, 11)
    key_key = jax.random.fold_in(key, 12)
    query_draw = jnp.clip(jax.random.normal(query_key, shape, jnp.float32), -6.0, 6.0)
    key_draw = jnp.clip(jax.random.normal(key_key, shape, jnp.float32), -6.0, 6.0)
    return (query_draw, key_draw)


def draw_queries(key, part):
    return drawn_pair(key)[0].astype(jnp.bfloat16)


def draw_keys(key, part):
    return drawn_pair(key)[1].astype(jnp.bfloat16)


def steps_of(key, extent, split, least, largest):
    loudness = 1.0
    for dim, shards_of in split:
        steps = jax.random.uniform(jax.random.fold_in(jax.random.fold_in(key, 6), dim), (shards_of,), jnp.float32, least / len(split), largest / len(split))
        loudness = loudness * jnp.repeat(jnp.exp(steps), extent[dim] // shards_of).reshape((-1,) + (1,) * (len(extent) - 1 - dim))
    return loudness


def scatter_about(own_key, extent, deviation, most, shards=(), held_as=jnp.bfloat16):
    array = jax.random.normal(own_key, extent, jnp.float32) * deviation
    if len(shards) > 0:
        array = steps_of(own_key, extent, shards, -0.22, 0.18) * array
    return jnp.clip(array, min=-most, max=most).astype(held_as)


def setup_inputs(seed: int = 0, part: int = 0) -> dict:
    key_of = jax.random.split(jax.random.key(seed), 4)
    part_keys = jax.random.split(jax.random.fold_in(key_of[3], part), 4)
    return {
        "queries": draw_queries(jax.random.fold_in(jax.random.fold_in(key_of[3], part), 71), part),
        "keys": draw_keys(jax.random.fold_in(jax.random.fold_in(key_of[3], part), 71), part),
        "values": scatter_about(part_keys[2], (BANDS, PATCHES, WIDTH), 1.0, 6.0, ((0, 8),)),
    }


def one_head(operands):
    query_head, key_head, value_head = operands
    row_count = query_head.shape[0]
    band_of = jnp.arange(row_count, dtype=jnp.int32) // PATCHES
    keep = band_of[:, None] >= band_of[None, :]
    scores = jnp.dot(query_head, key_head.T, preferred_element_type=jnp.float32) * (HDIM ** -0.5)
    scores = jnp.where(keep, scores, jnp.float32(-1e30))
    row_max = jnp.max(scores, axis=1, keepdims=True)
    weights = jnp.where(keep, jnp.exp(scores - row_max), jnp.float32(0.0))
    totals = jnp.sum(weights, axis=1, keepdims=True)
    summed = jnp.dot(weights.astype(jnp.bfloat16), value_head, preferred_element_type=jnp.float32)
    return summed / totals


def reference(queries, keys, values):
    row_count = BANDS * PATCHES
    query_heads = queries.reshape(row_count, HEADS, HDIM).transpose(1, 0, 2)
    key_heads = keys.reshape(row_count, HEADS, HDIM).transpose(1, 0, 2)
    value_heads = values.reshape(row_count, HEADS, HDIM).transpose(1, 0, 2)
    outputs = lax.map(one_head, (query_heads, key_heads, value_heads))
    return outputs.transpose(1, 0, 2).reshape(BANDS, PATCHES, HEADS * HDIM).astype(jnp.bfloat16)
```

```python
import functools
import math

import jax
import jax.numpy as jnp
from jax import lax
from jax.experimental import pallas as pl
from jax.experimental.pallas import tpu as pltpu
from jax.sharding import PartitionSpec as P

HDIM = 128
MESH = pl.DeviceIdType.MESH
SCALE = HDIM ** (-0.5) * math.log2(math.e)


def softmax_block(q, k, v, keep=None):
    s = lax.dot_general(q, k, (((1,), (1,)), ((), ())), preferred_element_type=jnp.float32)
    if keep is not None:
        s = jnp.where(keep, s, jnp.float32(-1e30))
    top = jnp.max(s, axis=1, keepdims=True)
    p = jnp.exp2((s - top) * SCALE)
    p = p.astype(jnp.bfloat16)
    ve = jnp.concatenate([v, jnp.ones_like(v)], axis=1)
    o = jnp.dot(p, ve, preferred_element_type=jnp.float32)
    total = o[:, HDIM:]
    return o[:, :HDIM] / total, top * SCALE + jnp.log2(total)


def kernel(
    chips, patches,
    q_hbm, k_hbm, v_hbm, o_ref,
    q_v, k_v, v_v, sib_k, sib_v, kall, vall, qall, out_p, out_s, part, stat, loc_o, loc_s,
    load_sem, own_sem, kv_send, kv_recv, q_send, q_recv, sib_send, sib_recv, sibh_send, sibh_recv,
    part_send, part_recv,
):
    rows, width = q_v.shape
    heads = width // HDIM
    half = heads // 2
    mid = chips // 2
    hub = mid - 1
    me = lax.axis_index("blk")
    z, c = me // 2, me % 2
    other = 1 - c
    sib = z * 2 + other
    lower = z < mid
    base = jnp.where(lower, z * (2 * rows), 0)

    def remote(src, dst, send, recv, dev):
        return pltpu.make_async_remote_copy(
            src_ref=src, dst_ref=dst, send_sem=send, recv_sem=recv,
            device_id={"blk": dev}, device_id_type=MESH,
        )

    def lanes(h):
        return pl.ds(pl.multiple_of(h * HDIM, HDIM), HDIM)

    def span(at, count=1):
        return pl.ds(pl.multiple_of(at, rows), count * rows)

    def each(lo, hi, body):
        def step(i, carry):
            body(i)
            return carry
        lax.fori_loop(lo, hi, step, 0)

    loads = [
        pltpu.make_async_copy(src, dst, load_sem.at[n])
        for n, (src, dst) in enumerate(((q_hbm, q_v), (k_hbm, k_v), (v_hbm, v_v)))
    ]
    for copy in loads:
        copy.start()
    own = []
    for h in range(half):
        at = lanes(c * half + h)
        own.append((
            pltpu.make_async_copy(k_hbm.at[:, at], kall.at[h, span(base + c * rows)], own_sem.at[h, 0]),
            pltpu.make_async_copy(v_hbm.at[:, at], vall.at[h, span(base + c * rows)], own_sem.at[h, 1]),
            pltpu.make_async_copy(q_hbm.at[:, at], qall.at[h, span((mid * 2 + c) * rows)], own_sem.at[h, 2]),
        ))
        for copy in own[-1]:
            copy.start()

    barrier = pltpu.get_barrier_semaphore()
    count = 2 * chips
    for step in range(1, count):
        pl.semaphore_signal(
            barrier, inc=1, device_id={"blk": lax.rem(me + step, count)}, device_id_type=MESH
        )
    pl.semaphore_wait(barrier, count - 1)
    for copy in loads:
        copy.wait()

    def kv_push(h, do):
        def to(j):
            for cc in range(2):
                at = lanes(cc * half + h)
                for n, (src, dst) in enumerate(((k_v, kall), (v_v, vall))):
                    do(remote(src.at[:, at], dst.at[h, span((z * 2 + c) * rows)],
                              kv_send.at[j, cc, h, n], kv_recv.at[z, c, h, n], j * 2 + cc))
        each(z + 1, jnp.where(lower, mid, 0), to)

    def q_push(h, do):
        def to(i):
            for cc in range(2):
                do(remote(q_v.at[:, lanes(cc * half + h)], qall.at[h, span(((z - mid) * 2 + c) * rows)],
                          q_send.at[i - hub, cc, h], q_recv.at[z - mid, c, h], i * 2 + cc))
        each(hub, jnp.where(lower, 0, z), to)

    def sib_push(h, do):
        at = lanes(other * half + h)
        for n, (src, dst, row) in enumerate((
            (k_v, kall, base + c * rows), (v_v, vall, base + c * rows), (q_v, qall, (mid * 2 + c) * rows),
        )):
            do(remote(src.at[:, at], dst.at[h, span(row)], sibh_send.at[h, n], sibh_recv.at[h, n], sib))

    def sib_whole(do):
        @pl.when(c == 0)
        def _():
            for n, (src, dst) in enumerate(((k_v, sib_k), (v_v, sib_v))):
                do(remote(src, dst, sib_send.at[n], sib_recv.at[n], sib))

    def start(copy):
        copy.start()

    def wait_send(copy):
        copy.wait_send()

    for h in range(half):
        kv_push(h, start)
        q_push(h, start)
        if h == 0:
            sib_whole(start)
        sib_push(h, start)

    row_band = lax.broadcasted_iota(jnp.int32, (rows, rows), 0) // patches
    key_band = lax.broadcasted_iota(jnp.int32, (rows, rows), 1) // patches
    keep = row_band >= key_band

    @pl.when(c == 0)
    def _():
        def body(h):
            at = lanes(h)
            loc_o[h], loc_s[h] = softmax_block(q_v[:, at], k_v[:, at], v_v[:, at], keep)
        each(0, heads, body)

    @pl.when(c == 1)
    def _():
        for n, dst in enumerate((sib_k, sib_v)):
            remote(dst, dst, sib_send.at[n], sib_recv.at[n], sib).wait_recv()
        keep2 = jnp.concatenate([keep, jnp.full((rows, rows), True)], axis=1)

        def body(h):
            at = lanes(h)
            loc_o[h], loc_s[h] = softmax_block(
                q_v[:, at],
                jnp.concatenate([k_v[:, at], sib_k[:, at]], axis=0),
                jnp.concatenate([v_v[:, at], sib_v[:, at]], axis=0),
                keep2,
            )
        each(0, heads, body)

    def block(q_slot, h, key_at, key_count):
        q = qall[h, span(q_slot * 2 * rows, 2), :]
        o, s = softmax_block(q, kall[h, key_at : key_at + key_count, :] if isinstance(key_at, int)
                             else kall[h, pl.ds(pl.multiple_of(key_at, rows), key_count), :],
                             vall[h, key_at : key_at + key_count, :] if isinstance(key_at, int)
                             else vall[h, pl.ds(pl.multiple_of(key_at, rows), key_count), :])
        return o.astype(jnp.bfloat16), s.T[0:1, :]

    def deliver(q_slot, h, slot, chip, cc, do):
        for n, (src, dst) in enumerate(((out_p, part), (out_s, stat))):
            do(remote(src.at[q_slot, cc, h], dst.at[slot, c * half + h],
                      part_send.at[q_slot, cc, h, n], part_recv.at[slot, c * half + h, n], chip * 2 + cc))

    def compute(q_slot, h, key_at, key_count, slot, chip):
        o, s = block(q_slot, h, key_at, key_count)
        for cc in range(2):
            out_p[q_slot, cc, h] = o[cc * rows : (cc + 1) * rows]
            out_s[q_slot, cc, h] = s[:, cc * rows : (cc + 1) * rows]
            deliver(q_slot, h, slot, chip, cc, start)

    def wait_local_kv(h):
        for n in range(2):
            own[h][n].wait()
        for n, dst in enumerate((kall, vall)):
            ref = dst.at[h, span(base + other * rows)]
            remote(ref, ref, sibh_send.at[h, n], sibh_recv.at[h, n], sib).wait_recv()

    def wait_own_q(h):
        own[h][2].wait()
        ref = qall.at[h, span((mid * 2 + other) * rows)]
        remote(ref, ref, sibh_send.at[h, 2], sibh_recv.at[h, 2], sib).wait_recv()

    def wait_q(j, h):
        for cc in range(2):
            ref = qall.at[h, span(((j - mid) * 2 + cc) * rows)]
            remote(ref, ref, q_send.at[0, cc, h], q_recv.at[j - mid, cc, h], sib).wait_recv()

    def wait_kv(i, h):
        for cc in range(2):
            for n, dst in enumerate((kall, vall)):
                ref = dst.at[h, span((i * 2 + cc) * rows)]
                remote(ref, ref, kv_send.at[0, cc, h, n], kv_recv.at[i, cc, h, n], sib).wait_recv()

    for h in range(half):
        wait_local_kv(h)
        wait_own_q(h)

        @pl.when(lower)
        def _():
            each(0, z, lambda i: wait_kv(i, h))

            @pl.when(z == hub)
            def _():
                def body(n):
                    j = chips - 1 - n
                    wait_q(j, h)
                    compute(j - mid, h, 0, 2 * mid * rows, 0, j)
                each(0, chips - mid, body)

            def body(i):
                o, s = block(mid, h, i * 2 * rows, 2 * rows)
                for cc in range(2):
                    @pl.when(cc == c)
                    def _():
                        part[i, c * half + h] = o[cc * rows : (cc + 1) * rows]
                        stat[i, c * half + h] = s[:, cc * rows : (cc + 1) * rows]

                    @pl.when(cc != c)
                    def _():
                        out_p[mid + i, cc, h] = o[cc * rows : (cc + 1) * rows]
                        out_s[mid + i, cc, h] = s[:, cc * rows : (cc + 1) * rows]
                        deliver(mid + i, h, i, z, cc, start)
            each(0, z, body)

        @pl.when(jnp.logical_not(lower))
        def _():
            def body(j):
                wait_q(j, h)
                compute(j - mid, h, 0, 2 * rows, 1 + z - mid, j)
            each(z + 1, chips, body)

    def finish(head, from_me):
        at = lanes(head)

        def merge(slot, carry):
            acc, weight, top = carry
            @pl.when(jnp.logical_not(jnp.logical_and(lower, from_me)))
            def _():
                for n, dst in enumerate((part, stat)):
                    ref = dst.at[slot, head]
                    remote(ref, ref, part_send.at[0, 0, 0, n], part_recv.at[slot, head, n], sib).wait_recv()
            s = jnp.broadcast_to(stat[slot, head], (HDIM, rows)).T
            new_top = jnp.maximum(top, s)
            a, b = jnp.exp2(top - new_top), jnp.exp2(s - new_top)
            return acc * a + part[slot, head].astype(jnp.float32) * b, weight * a + b, new_top

        acc, weight, _ = lax.fori_loop(
            0, jnp.where(lower, z, z - mid + 1), merge,
            (loc_o[head], jnp.ones((rows, HDIM), jnp.float32), loc_s[head]),
        )
        o_ref[:, at] = (acc / weight).astype(o_ref.dtype)

    for h in range(half):
        for cc in range(2):
            finish(cc * half + h, cc == c)

    for h in range(half):
        kv_push(h, wait_send)
        q_push(h, wait_send)
        sib_push(h, wait_send)

        @pl.when(z == hub)
        def _():
            def body(j):
                for cc in range(2):
                    deliver(j - mid, h, 0, j, cc, wait_send)
            each(mid, chips, body)

        @pl.when(lower)
        def _():
            each(0, z, lambda i: deliver(mid + i, h, i, z, other, wait_send))

        @pl.when(jnp.logical_not(lower))
        def _():
            def body(j):
                for cc in range(2):
                    deliver(j - mid, h, 1 + z - mid, j, cc, wait_send)
            each(z + 1, chips, body)
    sib_whole(wait_send)


def shards(chips, queries, keys, values):
    band_count, patch_count, width = queries.shape
    rows = band_count * patch_count
    heads = width // HDIM
    half = heads // 2
    mid = chips // 2
    bf16, f32 = jnp.bfloat16, jnp.float32
    dma = pltpu.SemaphoreType.DMA
    out = pl.pallas_call(
        functools.partial(kernel, chips, patch_count),
        out_shape=jax.ShapeDtypeStruct((rows, width), bf16),
        in_specs=[pl.BlockSpec(memory_space=pl.ANY)] * 3,
        out_specs=pl.BlockSpec(memory_space=pltpu.VMEM),
        scratch_shapes=[
            pltpu.VMEM((rows, width), bf16),
            pltpu.VMEM((rows, width), bf16),
            pltpu.VMEM((rows, width), bf16),
            pltpu.VMEM((rows, width), bf16),
            pltpu.VMEM((rows, width), bf16),
            pltpu.VMEM((half, 2 * mid * rows, HDIM), bf16),
            pltpu.VMEM((half, 2 * mid * rows, HDIM), bf16),
            pltpu.VMEM((half, 2 * (mid + 1) * rows, HDIM), bf16),
            pltpu.VMEM((2 * mid, 2, half, rows, HDIM), bf16),
            pltpu.VMEM((2 * mid, 2, half, 1, rows), f32),
            pltpu.VMEM((mid, heads, rows, HDIM), bf16),
            pltpu.VMEM((mid, heads, 1, rows), f32),
            pltpu.VMEM((heads, rows, HDIM), f32),
            pltpu.VMEM((heads, rows, HDIM), f32),
            dma((3,)),
            dma((half, 3)),
            dma((mid, 2, half, 2)),
            dma((mid, 2, half, 2)),
            dma((mid, 2, half)),
            dma((mid, 2, half)),
            dma((2,)),
            dma((2,)),
            dma((half, 3)),
            dma((half, 3)),
            dma((2 * mid, 2, half, 2)),
            dma((mid, heads, 2)),
        ],
        compiler_params=pltpu.CompilerParams(
            collective_id=0, has_side_effects=True, vmem_limit_bytes=48 * 1024 * 1024
        ),
        cost_estimate=pl.CostEstimate(
            flops=4 * rows * chips * rows * width, bytes_accessed=8 * rows * width, transcendentals=0
        ),
    )(*(a.reshape(rows, width) for a in (queries, keys, values)))
    return out.reshape(band_count, patch_count, width)


def solution(mesh):
    spec = P(("dp", "blk"), None, None)
    return jax.shard_map(
        functools.partial(shards, mesh.shape["blk"] // 2),
        mesh=mesh,
        in_specs=(spec, spec, spec),
        out_specs=spec,
        check_vma=False,
    )
```

```python
import functools
import math

import jax
import jax.numpy as jnp
from jax import lax
from jax.experimental import pallas as pl
from jax.experimental.pallas import tpu as pltpu
from jax.sharding import PartitionSpec as P

HDIM = 128
MESH = pl.DeviceIdType.MESH
WINDOW = 3
SCALE = HDIM ** (-0.5) * math.log2(math.e)


def softmax_block(q, k, v, keep=None):
    s = lax.dot_general(q, k, (((1,), (1,)), ((), ())), preferred_element_type=jnp.float32)
    if keep is not None:
        s = jnp.where(keep, s, jnp.float32(-1e30))
    top = jnp.max(s, axis=1, keepdims=True)
    p = jnp.exp2((s - top) * SCALE)
    p = p.astype(jnp.bfloat16)
    ve = jnp.concatenate([v, jnp.ones_like(v)], axis=1)
    o = jnp.dot(p, ve, preferred_element_type=jnp.float32)
    total = o[:, HDIM:]
    return o[:, :HDIM] / total, top * SCALE + jnp.log2(total)


def kernel(
    chips, patches,
    q_hbm, k_hbm, v_hbm, o_hbm,
    o_v, q_v, k_v, v_v, sib_k, sib_v, kall, vall, qall, out_p, out_s, part, stat, loc_o, loc_s,
    load_sem, own_sem, kv_send, kv_recv, q_send, q_recv, sib_send, sib_recv, sibh_send, sibh_recv,
    part_send, part_recv, out_sem,
):
    rows, width = q_v.shape
    heads = width // HDIM
    half = heads // 2
    mid = chips // 2
    hub = mid - 1
    me = lax.axis_index("blk")
    z, c = me // 2, me % 2
    other = 1 - c
    sib = z * 2 + other
    lower = z < mid
    base = jnp.where(lower, z * (2 * rows), 0)

    def remote(src, dst, send, recv, dev):
        return pltpu.make_async_remote_copy(
            src_ref=src, dst_ref=dst, send_sem=send, recv_sem=recv,
            device_id={"blk": dev}, device_id_type=MESH,
        )

    def lanes(h):
        return pl.ds(pl.multiple_of(h * HDIM, HDIM), HDIM)

    def span(at, count=1):
        return pl.ds(pl.multiple_of(at, rows), count * rows)

    def each(lo, hi, body):
        def step(i, carry):
            body(i)
            return carry
        lax.fori_loop(lo, hi, step, 0)

    loads = [
        pltpu.make_async_copy(src, dst, load_sem.at[n])
        for n, (src, dst) in enumerate(((q_hbm, q_v), (k_hbm, k_v), (v_hbm, v_v)))
    ]
    for copy in loads:
        copy.start()
    own = []
    for h in range(half):
        at = lanes(c * half + h)
        own.append((
            pltpu.make_async_copy(k_hbm.at[:, at], kall.at[h, span(base + c * rows)], own_sem.at[h, 0]),
            pltpu.make_async_copy(v_hbm.at[:, at], vall.at[h, span(base + c * rows)], own_sem.at[h, 1]),
            pltpu.make_async_copy(q_hbm.at[:, at], qall.at[h, span((mid * 2 + c) * rows)], own_sem.at[h, 2]),
        ))
        for copy in own[-1]:
            copy.start()

    barrier = pltpu.get_barrier_semaphore()
    count = 2 * chips
    for step in range(1, count):
        dev = lax.rem(me + step, count)
        y = dev // 2

        @pl.when((lower & (y < mid)) | ((z >= mid) & (y >= mid)) | (z == hub) | (y == hub))
        def _():
            pl.semaphore_signal(barrier, inc=1, device_id={"blk": dev}, device_id_type=MESH)
    pl.semaphore_wait(barrier, jnp.where(
        z == hub, count - 1, jnp.where(lower, 2 * mid - 1, 2 * (chips - mid) + 1)
    ))

    def kv_push(h, cc, do):
        def to(j):
            at = lanes(cc * half + h)
            for n, (src, dst) in enumerate(((k_hbm, kall), (v_hbm, vall))):
                do(remote(src.at[:, at], dst.at[h, span((z * 2 + c) * rows)],
                          kv_send.at[j, cc, h, n], kv_recv.at[z, c, h, n], j * 2 + cc))
        each(z + 1, jnp.where(lower, mid, 0), to)

    def q_push(h, cc, do):
        def to(i):
            do(remote(q_hbm.at[:, lanes(cc * half + h)], qall.at[h, span(((z - mid) * 2 + c) * rows)],
                      q_send.at[i - hub, cc, h], q_recv.at[z - mid, c, h], i * 2 + cc))
        each(hub, jnp.where(lower, 0, z), to)

    def push(item, do):
        h, cc = item // 2, item % 2
        kv_push(h, cc, do)
        q_push(h, cc, do)

    def sib_push(h, do):
        at = lanes(other * half + h)
        for n, (src, dst, row) in enumerate((
            (k_v, kall, base + c * rows), (v_v, vall, base + c * rows), (q_v, qall, (mid * 2 + c) * rows),
        )):
            do(remote(src.at[:, at], dst.at[h, span(row)], sibh_send.at[h, n], sibh_recv.at[h, n], sib))

    def sib_whole(do):
        @pl.when(c == 0)
        def _():
            for n, (src, dst) in enumerate(((k_v, sib_k), (v_v, sib_v))):
                do(remote(src, dst, sib_send.at[n], sib_recv.at[n], sib))

    def start(copy):
        copy.start()

    def wait_send(copy):
        copy.wait_send()

    for item in range(min(WINDOW, heads)):
        push(item, start)
    for copy in loads:
        copy.wait()
    sib_whole(start)
    for h in range(half):
        sib_push(h, start)

    row_band = lax.broadcasted_iota(jnp.int32, (rows, rows), 0) // patches
    key_band = lax.broadcasted_iota(jnp.int32, (rows, rows), 1) // patches
    keep = row_band >= key_band

    keep2 = jnp.concatenate([keep, jnp.full((rows, rows), True)], axis=1)

    @pl.when(c == 1)
    def _():
        for n, dst in enumerate((sib_k, sib_v)):
            remote(dst, dst, sib_send.at[n], sib_recv.at[n], sib).wait_recv()

    def attend_local(h):
        at = lanes(h)

        @pl.when(c == 0)
        def _():
            loc_o[h], loc_s[h] = softmax_block(q_v[:, at], k_v[:, at], v_v[:, at], keep)

        @pl.when(c == 1)
        def _():
            loc_o[h], loc_s[h] = softmax_block(
                q_v[:, at],
                jnp.concatenate([k_v[:, at], sib_k[:, at]], axis=0),
                jnp.concatenate([v_v[:, at], sib_v[:, at]], axis=0),
                keep2,
            )

    def block(q_slot, h, key_at, key_count):
        q = qall[h, span(q_slot * 2 * rows, 2), :]
        o, s = softmax_block(q, kall[h, key_at : key_at + key_count, :] if isinstance(key_at, int)
                             else kall[h, pl.ds(pl.multiple_of(key_at, rows), key_count), :],
                             vall[h, key_at : key_at + key_count, :] if isinstance(key_at, int)
                             else vall[h, pl.ds(pl.multiple_of(key_at, rows), key_count), :])
        return o.astype(jnp.bfloat16), s.T[0:1, :]

    def deliver(q_slot, h, slot, chip, cc, do):
        for n, (src, dst) in enumerate(((out_p, part), (out_s, stat))):
            do(remote(src.at[q_slot, cc, h], dst.at[slot, c * half + h],
                      part_send.at[q_slot, cc, h, n], part_recv.at[slot, c * half + h, n], chip * 2 + cc))

    def compute(q_slot, h, key_at, key_count, slot, chip):
        o, s = block(q_slot, h, key_at, key_count)
        for cc in range(2):
            out_p[q_slot, cc, h] = o[cc * rows : (cc + 1) * rows]
            out_s[q_slot, cc, h] = s[:, cc * rows : (cc + 1) * rows]
            deliver(q_slot, h, slot, chip, cc, start)

    def wait_local_kv(h):
        for n in range(2):
            own[h][n].wait()
        for n, dst in enumerate((kall, vall)):
            ref = dst.at[h, span(base + other * rows)]
            remote(ref, ref, sibh_send.at[h, n], sibh_recv.at[h, n], sib).wait_recv()

    def wait_own_q(h):
        own[h][2].wait()
        ref = qall.at[h, span((mid * 2 + other) * rows)]
        remote(ref, ref, sibh_send.at[h, 2], sibh_recv.at[h, 2], sib).wait_recv()

    def wait_q(j, h):
        for cc in range(2):
            ref = qall.at[h, span(((j - mid) * 2 + cc) * rows)]
            remote(ref, ref, q_send.at[0, cc, h], q_recv.at[j - mid, cc, h], sib).wait_recv()

    def wait_kv(i, h):
        for cc in range(2):
            for n, dst in enumerate((kall, vall)):
                ref = dst.at[h, span((i * 2 + cc) * rows)]
                remote(ref, ref, kv_send.at[0, cc, h, n], kv_recv.at[i, cc, h, n], sib).wait_recv()

    for item in range(heads):
        h = item // 2
        attend_local(item)
        if item + WINDOW < heads:
            push(item, wait_send)
            push(item + WINDOW, start)
        if item % 2 == 1:
            wait_local_kv(h)
            wait_own_q(h)

            @pl.when(jnp.logical_not(lower))
            def _():
                def body(j):
                    wait_q(j, h)
                    compute(j - mid, h, 0, 2 * rows, 1 + z - mid, j)
                each(z + 1, chips, body)

    for h in range(half):
        @pl.when(lower)
        def _():
            each(0, z, lambda i: wait_kv(i, h))

            @pl.when(z == hub)
            def _():
                def body(n):
                    j = chips - 1 - n
                    wait_q(j, h)
                    compute(j - mid, h, 0, 2 * mid * rows, 0, j)
                each(0, chips - mid, body)

            def body(i):
                o, s = block(mid, h, i * 2 * rows, 2 * rows)
                for cc in range(2):
                    @pl.when(cc == c)
                    def _():
                        part[i, c * half + h] = o[cc * rows : (cc + 1) * rows]
                        stat[i, c * half + h] = s[:, cc * rows : (cc + 1) * rows]

                    @pl.when(cc != c)
                    def _():
                        out_p[mid + i, cc, h] = o[cc * rows : (cc + 1) * rows]
                        out_s[mid + i, cc, h] = s[:, cc * rows : (cc + 1) * rows]
                        deliver(mid + i, h, i, z, cc, start)
            each(0, z, body)

    def out_copy(head):
        at = lanes(head)
        return pltpu.make_async_copy(o_v.at[:, at], o_hbm.at[:, at], out_sem.at[head])

    def finish(head, from_me):
        at = lanes(head)

        def merge(slot, carry):
            acc, weight, top = carry
            @pl.when(jnp.logical_not(jnp.logical_and(lower, from_me)))
            def _():
                for n, dst in enumerate((part, stat)):
                    ref = dst.at[slot, head]
                    remote(ref, ref, part_send.at[0, 0, 0, n], part_recv.at[slot, head, n], sib).wait_recv()
            s = jnp.broadcast_to(stat[slot, head], (HDIM, rows)).T
            new_top = jnp.maximum(top, s)
            a, b = jnp.exp2(top - new_top), jnp.exp2(s - new_top)
            return acc * a + part[slot, head].astype(jnp.float32) * b, weight * a + b, new_top

        acc, weight, _ = lax.fori_loop(
            0, jnp.where(lower, z, z - mid + 1), merge,
            (loc_o[head], jnp.ones((rows, HDIM), jnp.float32), loc_s[head]),
        )
        o_v[:, at] = (acc / weight).astype(o_v.dtype)
        out_copy(head).start()

    for h in range(half):
        for cc in range(2):
            finish(cc * half + h, cc == c)

    for item in range(max(heads - WINDOW, 0), heads):
        push(item, wait_send)
    for head in range(heads):
        out_copy(head).wait()
    for h in range(half):
        sib_push(h, wait_send)

        @pl.when(z == hub)
        def _():
            def body(j):
                for cc in range(2):
                    deliver(j - mid, h, 0, j, cc, wait_send)
            each(mid, chips, body)

        @pl.when(lower)
        def _():
            each(0, z, lambda i: deliver(mid + i, h, i, z, other, wait_send))

        @pl.when(jnp.logical_not(lower))
        def _():
            def body(j):
                for cc in range(2):
                    deliver(j - mid, h, 1 + z - mid, j, cc, wait_send)
            each(z + 1, chips, body)
    sib_whole(wait_send)


def shards(chips, queries, keys, values):
    band_count, patch_count, width = queries.shape
    rows = band_count * patch_count
    heads = width // HDIM
    half = heads // 2
    mid = chips // 2
    bf16, f32 = jnp.bfloat16, jnp.float32
    dma = pltpu.SemaphoreType.DMA
    out = pl.pallas_call(
        functools.partial(kernel, chips, patch_count),
        out_shape=jax.ShapeDtypeStruct((rows, width), bf16),
        in_specs=[pl.BlockSpec(memory_space=pl.ANY)] * 3,
        out_specs=pl.BlockSpec(memory_space=pl.ANY),
        scratch_shapes=[
            pltpu.VMEM((rows, width), bf16),
            pltpu.VMEM((rows, width), bf16),
            pltpu.VMEM((rows, width), bf16),
            pltpu.VMEM((rows, width), bf16),
            pltpu.VMEM((rows, width), bf16),
            pltpu.VMEM((rows, width), bf16),
            pltpu.VMEM((half, 2 * mid * rows, HDIM), bf16),
            pltpu.VMEM((half, 2 * mid * rows, HDIM), bf16),
            pltpu.VMEM((half, 2 * (mid + 1) * rows, HDIM), bf16),
            pltpu.VMEM((2 * mid, 2, half, rows, HDIM), bf16),
            pltpu.VMEM((2 * mid, 2, half, 1, rows), f32),
            pltpu.VMEM((mid, heads, rows, HDIM), bf16),
            pltpu.VMEM((mid, heads, 1, rows), f32),
            pltpu.VMEM((heads, rows, HDIM), f32),
            pltpu.VMEM((heads, rows, HDIM), f32),
            dma((3,)),
            dma((half, 3)),
            dma((mid, 2, half, 2)),
            dma((mid, 2, half, 2)),
            dma((mid, 2, half)),
            dma((mid, 2, half)),
            dma((2,)),
            dma((2,)),
            dma((half, 3)),
            dma((half, 3)),
            dma((2 * mid, 2, half, 2)),
            dma((mid, heads, 2)),
            dma((heads,)),
        ],
        compiler_params=pltpu.CompilerParams(
            collective_id=0, has_side_effects=True, vmem_limit_bytes=62 * 1024 * 1024
        ),
        cost_estimate=pl.CostEstimate(
            flops=4 * rows * chips * rows * width, bytes_accessed=8 * rows * width, transcendentals=0
        ),
    )(*(a.reshape(rows, width) for a in (queries, keys, values)))
    return out.reshape(band_count, patch_count, width)


def solution(mesh):
    spec = P(("dp", "blk"), None, None)
    return jax.shard_map(
        functools.partial(shards, mesh.shape["blk"] // 2),
        mesh=mesh,
        in_specs=(spec, spec, spec),
        out_specs=spec,
        check_vma=False,
    )
```

```python
import functools
import math

import jax
import jax.numpy as jnp
from jax import lax
from jax.experimental import pallas as pl
from jax.experimental.pallas import tpu as pltpu
from jax.sharding import PartitionSpec as P

HDIM = 128
MESH = pl.DeviceIdType.MESH
WINDOW = 3
SCALE = HDIM ** (-0.5) * math.log2(math.e)


def softmax_block(q, k, v, keep=None):
    s = lax.dot_general(q, k, (((1,), (1,)), ((), ())), preferred_element_type=jnp.float32)
    if keep is not None:
        s = jnp.where(keep, s, jnp.float32(-1e30))
    top = jnp.max(s, axis=1, keepdims=True)
    p = jnp.exp2((s - top) * SCALE)
    p = p.astype(jnp.bfloat16)
    ve = jnp.concatenate([v, jnp.ones_like(v)], axis=1)
    o = jnp.dot(p, ve, preferred_element_type=jnp.float32)
    total = o[:, HDIM:]
    return o[:, :HDIM] / total, top * SCALE + jnp.log2(total)


def kernel(
    chips, patches,
    q_hbm, k_hbm, v_hbm, o_hbm,
    o_v, q_v, k_v, v_v, sib_k, sib_v, kall, vall, qall, out_p, out_s, part, stat, loc_o, loc_s,
    load_sem, own_sem, kv_send, kv_recv, q_send, q_recv, sib_send, sib_recv, sibh_send, sibh_recv,
    part_send, part_recv, out_sem,
):
    rows, width = q_v.shape
    heads = width // HDIM
    half = heads // 2
    mid = chips // 2
    hub = mid - 1
    me = lax.axis_index("blk")
    z, c = me // 2, me % 2
    other = 1 - c
    sib = z * 2 + other
    lower = z < mid
    base = jnp.where(lower, z * (2 * rows), 0)

    def remote(src, dst, send, recv, dev):
        return pltpu.make_async_remote_copy(
            src_ref=src, dst_ref=dst, send_sem=send, recv_sem=recv,
            device_id={"blk": dev}, device_id_type=MESH,
        )

    def lanes(h):
        return pl.ds(pl.multiple_of(h * HDIM, HDIM), HDIM)

    def span(at, count=1):
        return pl.ds(pl.multiple_of(at, rows), count * rows)

    def each(lo, hi, body):
        def step(i, carry):
            body(i)
            return carry
        lax.fori_loop(lo, hi, step, 0)

    loads = [
        pltpu.make_async_copy(src, dst, load_sem.at[n])
        for n, (src, dst) in enumerate(((q_hbm, q_v), (k_hbm, k_v), (v_hbm, v_v)))
    ]
    for copy in loads:
        copy.start()
    own = []
    for h in range(half):
        at = lanes(c * half + h)
        own.append((
            pltpu.make_async_copy(k_hbm.at[:, at], kall.at[h, span(base + c * rows)], own_sem.at[h, 0]),
            pltpu.make_async_copy(v_hbm.at[:, at], vall.at[h, span(base + c * rows)], own_sem.at[h, 1]),
            pltpu.make_async_copy(q_hbm.at[:, at], qall.at[h, span((mid * 2 + c) * rows)], own_sem.at[h, 2]),
        ))
        for copy in own[-1]:
            copy.start()

    barrier = pltpu.get_barrier_semaphore()
    count = 2 * chips
    for step in range(1, count):
        dev = lax.rem(me + step, count)
        y = dev // 2

        @pl.when((lower & (y < mid)) | ((z >= mid) & (y >= mid)) | (z == hub) | (y == hub))
        def _():
            pl.semaphore_signal(barrier, inc=1, device_id={"blk": dev}, device_id_type=MESH)
    pl.semaphore_wait(barrier, jnp.where(
        z == hub, count - 1, jnp.where(lower, 2 * mid - 1, 2 * (chips - mid) + 1)
    ))

    def kv_push(h, cc, do):
        def to(j):
            at = lanes(cc * half + h)
            for n, (src, dst) in enumerate(((k_hbm, kall), (v_hbm, vall))):
                do(remote(src.at[:, at], dst.at[h, span((z * 2 + c) * rows)],
                          kv_send.at[j, cc, h, n], kv_recv.at[z, c, h, n], j * 2 + cc))
        each(z + 1, jnp.where(lower, mid, 0), to)

    def q_push(h, cc, do):
        def to(i):
            do(remote(q_hbm.at[:, lanes(cc * half + h)], qall.at[h, span(((z - mid) * 2 + c) * rows)],
                      q_send.at[i - hub, cc, h], q_recv.at[z - mid, c, h], i * 2 + cc))
        each(hub, jnp.where(lower, 0, z), to)

    def push(item, do):
        h, cc = item // 2, item % 2
        kv_push(h, cc, do)
        q_push(h, cc, do)

    def sib_push(h, do):
        at = lanes(other * half + h)
        for n, (src, dst, row) in enumerate((
            (k_v, kall, base + c * rows), (v_v, vall, base + c * rows), (q_v, qall, (mid * 2 + c) * rows),
        )):
            do(remote(src.at[:, at], dst.at[h, span(row)], sibh_send.at[h, n], sibh_recv.at[h, n], sib))

    def sib_whole(do):
        @pl.when(c == 0)
        def _():
            for n, (src, dst) in enumerate(((k_v, sib_k), (v_v, sib_v))):
                do(remote(src, dst, sib_send.at[n], sib_recv.at[n], sib))

    def start(copy):
        copy.start()

    def wait_send(copy):
        copy.wait_send()

    for item in range(min(WINDOW, heads)):
        push(item, start)
    for copy in loads:
        copy.wait()
    for h in range(half):
        sib_push(h, start)
    sib_whole(start)

    row_band = lax.broadcasted_iota(jnp.int32, (rows, rows), 0) // patches
    key_band = lax.broadcasted_iota(jnp.int32, (rows, rows), 1) // patches
    keep = row_band >= key_band

    keep2 = jnp.concatenate([keep, jnp.full((rows, rows), True)], axis=1)

    def attend_local(h):
        at = lanes(h)

        @pl.when(c == 0)
        def _():
            loc_o[h], loc_s[h] = softmax_block(q_v[:, at], k_v[:, at], v_v[:, at], keep)

        @pl.when(c == 1)
        def _():
            loc_o[h], loc_s[h] = softmax_block(
                q_v[:, at],
                jnp.concatenate([k_v[:, at], sib_k[:, at]], axis=0),
                jnp.concatenate([v_v[:, at], sib_v[:, at]], axis=0),
                keep2,
            )

    def block(q_slot, h, key_at, key_count):
        q = qall[h, span(q_slot * 2 * rows, 2), :]
        o, s = softmax_block(q, kall[h, key_at : key_at + key_count, :] if isinstance(key_at, int)
                             else kall[h, pl.ds(pl.multiple_of(key_at, rows), key_count), :],
                             vall[h, key_at : key_at + key_count, :] if isinstance(key_at, int)
                             else vall[h, pl.ds(pl.multiple_of(key_at, rows), key_count), :])
        return o.astype(jnp.bfloat16), s.T[0:1, :]

    def deliver(q_slot, h, slot, chip, cc, do):
        for n, (src, dst) in enumerate(((out_p, part), (out_s, stat))):
            do(remote(src.at[q_slot, cc, h], dst.at[slot, c * half + h],
                      part_send.at[q_slot, cc, h, n], part_recv.at[slot, c * half + h, n], chip * 2 + cc))

    def compute(q_slot, h, key_at, key_count, slot, chip):
        o, s = block(q_slot, h, key_at, key_count)
        for cc in range(2):
            out_p[q_slot, cc, h] = o[cc * rows : (cc + 1) * rows]
            out_s[q_slot, cc, h] = s[:, cc * rows : (cc + 1) * rows]
            deliver(q_slot, h, slot, chip, cc, start)

    def wait_local_kv(h):
        for n in range(2):
            own[h][n].wait()
        for n, dst in enumerate((kall, vall)):
            ref = dst.at[h, span(base + other * rows)]
            remote(ref, ref, sibh_send.at[h, n], sibh_recv.at[h, n], sib).wait_recv()

    def wait_own_q(h):
        own[h][2].wait()
        ref = qall.at[h, span((mid * 2 + other) * rows)]
        remote(ref, ref, sibh_send.at[h, 2], sibh_recv.at[h, 2], sib).wait_recv()

    def wait_q(j, h):
        for cc in range(2):
            ref = qall.at[h, span(((j - mid) * 2 + cc) * rows)]
            remote(ref, ref, q_send.at[0, cc, h], q_recv.at[j - mid, cc, h], sib).wait_recv()

    def wait_kv(i, h):
        for cc in range(2):
            for n, dst in enumerate((kall, vall)):
                ref = dst.at[h, span((i * 2 + cc) * rows)]
                remote(ref, ref, kv_send.at[0, cc, h, n], kv_recv.at[i, cc, h, n], sib).wait_recv()

    for item in range(heads):
        h = item // 2
        if item + WINDOW < heads:
            push(item, wait_send)
            push(item + WINDOW, start)
        if item % 2 == 0:
            wait_local_kv(h)
            wait_own_q(h)

            @pl.when(lower)
            def _():
                each(0, z, lambda i: wait_kv(i, h))

                @pl.when(z == hub)
                def _():
                    def body(n):
                        j = chips - 1 - n
                        wait_q(j, h)
                        compute(j - mid, h, 0, 2 * mid * rows, 0, j)
                    each(0, chips - mid, body)

                def body(i):
                    o, s = block(mid, h, i * 2 * rows, 2 * rows)
                    for cc in range(2):
                        @pl.when(cc == c)
                        def _():
                            part[i, c * half + h] = o[cc * rows : (cc + 1) * rows]
                            stat[i, c * half + h] = s[:, cc * rows : (cc + 1) * rows]

                        @pl.when(cc != c)
                        def _():
                            out_p[mid + i, cc, h] = o[cc * rows : (cc + 1) * rows]
                            out_s[mid + i, cc, h] = s[:, cc * rows : (cc + 1) * rows]
                            deliver(mid + i, h, i, z, cc, start)
                each(0, z, body)

        if item == 0:
            @pl.when(c == 1)
            def _():
                for n, dst in enumerate((sib_k, sib_v)):
                    remote(dst, dst, sib_send.at[n], sib_recv.at[n], sib).wait_recv()
        attend_local(item)
        if item % 2 == 1:
            @pl.when(jnp.logical_not(lower))
            def _():
                def body(j):
                    wait_q(j, h)
                    compute(j - mid, h, 0, 2 * rows, 1 + z - mid, j)
                each(z + 1, chips, body)

    def out_copy(head):
        at = lanes(head)
        return pltpu.make_async_copy(o_v.at[:, at], o_hbm.at[:, at], out_sem.at[head])

    def finish(head, from_me):
        at = lanes(head)

        def merge(slot, carry):
            acc, weight, top = carry
            @pl.when(jnp.logical_not(jnp.logical_and(lower, from_me)))
            def _():
                for n, dst in enumerate((part, stat)):
                    ref = dst.at[slot, head]
                    remote(ref, ref, part_send.at[0, 0, 0, n], part_recv.at[slot, head, n], sib).wait_recv()
            s = jnp.broadcast_to(stat[slot, head], (HDIM, rows)).T
            new_top = jnp.maximum(top, s)
            a, b = jnp.exp2(top - new_top), jnp.exp2(s - new_top)
            return acc * a + part[slot, head].astype(jnp.float32) * b, weight * a + b, new_top

        acc, weight, _ = lax.fori_loop(
            0, jnp.where(lower, z, z - mid + 1), merge,
            (loc_o[head], jnp.ones((rows, HDIM), jnp.float32), loc_s[head]),
        )
        o_v[:, at] = (acc / weight).astype(o_v.dtype)
        out_copy(head).start()

    for h in range(half):
        for cc in range(2):
            finish(cc * half + h, cc == c)

    for item in range(max(heads - WINDOW, 0), heads):
        push(item, wait_send)
    for head in range(heads):
        out_copy(head).wait()
    for h in range(half):
        sib_push(h, wait_send)

        @pl.when(z == hub)
        def _():
            def body(j):
                for cc in range(2):
                    deliver(j - mid, h, 0, j, cc, wait_send)
            each(mid, chips, body)

        @pl.when(lower)
        def _():
            each(0, z, lambda i: deliver(mid + i, h, i, z, other, wait_send))

        @pl.when(jnp.logical_not(lower))
        def _():
            def body(j):
                for cc in range(2):
                    deliver(j - mid, h, 1 + z - mid, j, cc, wait_send)
            each(z + 1, chips, body)
    sib_whole(wait_send)


def shards(chips, queries, keys, values):
    band_count, patch_count, width = queries.shape
    rows = band_count * patch_count
    heads = width // HDIM
    half = heads // 2
    mid = chips // 2
    bf16, f32 = jnp.bfloat16, jnp.float32
    dma = pltpu.SemaphoreType.DMA
    out = pl.pallas_call(
        functools.partial(kernel, chips, patch_count),
        out_shape=jax.ShapeDtypeStruct((rows, width), bf16),
        in_specs=[pl.BlockSpec(memory_space=pl.ANY)] * 3,
        out_specs=pl.BlockSpec(memory_space=pl.ANY),
        scratch_shapes=[
            pltpu.VMEM((rows, width), bf16),
            pltpu.VMEM((rows, width), bf16),
            pltpu.VMEM((rows, width), bf16),
            pltpu.VMEM((rows, width), bf16),
            pltpu.VMEM((rows, width), bf16),
            pltpu.VMEM((rows, width), bf16),
            pltpu.VMEM((half, 2 * mid * rows, HDIM), bf16),
            pltpu.VMEM((half, 2 * mid * rows, HDIM), bf16),
            pltpu.VMEM((half, 2 * (mid + 1) * rows, HDIM), bf16),
            pltpu.VMEM((2 * mid, 2, half, rows, HDIM), bf16),
            pltpu.VMEM((2 * mid, 2, half, 1, rows), f32),
            pltpu.VMEM((mid, heads, rows, HDIM), bf16),
            pltpu.VMEM((mid, heads, 1, rows), f32),
            pltpu.VMEM((heads, rows, HDIM), f32),
            pltpu.VMEM((heads, rows, HDIM), f32),
            dma((3,)),
            dma((half, 3)),
            dma((mid, 2, half, 2)),
            dma((mid, 2, half, 2)),
            dma((mid, 2, half)),
            dma((mid, 2, half)),
            dma((2,)),
            dma((2,)),
            dma((half, 3)),
            dma((half, 3)),
            dma((2 * mid, 2, half, 2)),
            dma((mid, heads, 2)),
            dma((heads,)),
        ],
        compiler_params=pltpu.CompilerParams(
            collective_id=0, has_side_effects=True, vmem_limit_bytes=62 * 1024 * 1024
        ),
        cost_estimate=pl.CostEstimate(
            flops=4 * rows * chips * rows * width, bytes_accessed=8 * rows * width, transcendentals=0
        ),
    )(*(a.reshape(rows, width) for a in (queries, keys, values)))
    return out.reshape(band_count, patch_count, width)


def solution(mesh):
    spec = P(("dp", "blk"), None, None)
    return jax.shard_map(
        functools.partial(shards, mesh.shape["blk"] // 2),
        mesh=mesh,
        in_specs=(spec, spec, spec),
        out_specs=spec,
        check_vma=False,
    )
```

```python
import functools
import math

import jax
import jax.numpy as jnp
from jax import lax
from jax.experimental import pallas as pl
from jax.experimental.pallas import tpu as pltpu
from jax.sharding import PartitionSpec as P

HDIM = 128
MESH = pl.DeviceIdType.MESH
WINDOW = 3
SCALE = HDIM ** (-0.5) * math.log2(math.e)


def softmax_block(q, k, v, keep=None):
    s = lax.dot_general(q, k, (((1,), (1,)), ((), ())), preferred_element_type=jnp.float32)
    if keep is not None:
        s = jnp.where(keep, s, jnp.float32(-1e30))
    top = jnp.max(s, axis=1, keepdims=True)
    p = jnp.exp2((s - top) * SCALE)
    p = p.astype(jnp.bfloat16)
    ve = jnp.concatenate([v, jnp.ones_like(v)], axis=1)
    o = jnp.dot(p, ve, preferred_element_type=jnp.float32)
    total = o[:, HDIM:]
    return o[:, :HDIM] / total, top * SCALE + jnp.log2(total)


def kernel(
    chips, patches,
    q_hbm, k_hbm, v_hbm, o_hbm,
    o_v, q_v, k_v, v_v, sib_k, sib_v, kall, vall, qall, out_p, out_s, part, stat, loc_o, loc_s,
    load_sem, own_sem, kv_send, kv_recv, q_send, q_recv, sib_send, sib_recv, sibh_send, sibh_recv,
    part_send, part_recv, out_sem,
):
    rows, width = q_v.shape
    heads = width // HDIM
    half = heads // 2
    mid = chips // 2
    hub = mid - 1
    me = lax.axis_index("blk")
    z, c = me // 2, me % 2
    other = 1 - c
    sib = z * 2 + other
    lower = z < mid
    base = jnp.where(lower, z * (2 * rows), 0)

    def remote(src, dst, send, recv, dev):
        return pltpu.make_async_remote_copy(
            src_ref=src, dst_ref=dst, send_sem=send, recv_sem=recv,
            device_id={"blk": dev}, device_id_type=MESH,
        )

    def lanes(h):
        return pl.ds(pl.multiple_of(h * HDIM, HDIM), HDIM)

    def span(at, count=1):
        return pl.ds(pl.multiple_of(at, rows), count * rows)

    def each(lo, hi, body):
        def step(i, carry):
            body(i)
            return carry
        lax.fori_loop(lo, hi, step, 0)

    loads = [
        pltpu.make_async_copy(src, dst, load_sem.at[n])
        for n, (src, dst) in enumerate(((q_hbm, q_v), (k_hbm, k_v), (v_hbm, v_v)))
    ]
    for copy in loads:
        copy.start()
    own = []
    for h in range(half):
        at = lanes(c * half + h)
        own.append((
            pltpu.make_async_copy(k_hbm.at[:, at], kall.at[h, span(base + c * rows)], own_sem.at[h, 0]),
            pltpu.make_async_copy(v_hbm.at[:, at], vall.at[h, span(base + c * rows)], own_sem.at[h, 1]),
            pltpu.make_async_copy(q_hbm.at[:, at], qall.at[h, span((mid * 2 + c) * rows)], own_sem.at[h, 2]),
        ))
        for copy in own[-1]:
            copy.start()

    barrier = pltpu.get_barrier_semaphore()
    count = 2 * chips
    for step in range(1, count):
        dev = lax.rem(me + step, count)
        y = dev // 2

        @pl.when((lower & (y < mid)) | ((z >= mid) & (y >= mid)) | (z == hub) | (y == hub))
        def _():
            pl.semaphore_signal(barrier, inc=1, device_id={"blk": dev}, device_id_type=MESH)
    pl.semaphore_wait(barrier, jnp.where(
        z == hub, count - 1, jnp.where(lower, 2 * mid - 1, 2 * (chips - mid) + 1)
    ))

    def kv_push(h, cc, do):
        def to(j):
            at = lanes(cc * half + h)
            for n, (src, dst) in enumerate(((k_hbm, kall), (v_hbm, vall))):
                do(remote(src.at[:, at], dst.at[h, span((z * 2 + c) * rows)],
                          kv_send.at[j, cc, h, n], kv_recv.at[z, c, h, n], j * 2 + cc))
        each(z + 1, jnp.where(lower, mid, 0), to)

    def q_push(h, cc, do):
        def to(i):
            do(remote(q_hbm.at[:, lanes(cc * half + h)], qall.at[h, span(((z - mid) * 2 + c) * rows)],
                      q_send.at[i - hub, cc, h], q_recv.at[z - mid, c, h], i * 2 + cc))
        each(hub, jnp.where(lower, 0, z), to)

    def push(item, do):
        h, cc = item // 2, item % 2
        kv_push(h, cc, do)
        q_push(h, cc, do)

    def sib_push(h, do):
        at = lanes(other * half + h)
        for n, (src, dst, row) in enumerate((
            (k_v, kall, base + c * rows), (v_v, vall, base + c * rows), (q_v, qall, (mid * 2 + c) * rows),
        )):
            do(remote(src.at[:, at], dst.at[h, span(row)], sibh_send.at[h, n], sibh_recv.at[h, n], sib))

    def sib_whole(do):
        @pl.when(c == 0)
        def _():
            for n, (src, dst) in enumerate(((k_v, sib_k), (v_v, sib_v))):
                do(remote(src, dst, sib_send.at[n], sib_recv.at[n], sib))

    def start(copy):
        copy.start()

    def wait_send(copy):
        copy.wait_send()

    for item in range(min(WINDOW, heads)):
        push(item, start)
    for copy in loads:
        copy.wait()
    for h in range(half):
        sib_push(h, start)
    sib_whole(start)

    row_band = lax.broadcasted_iota(jnp.int32, (rows, rows), 0) // patches
    key_band = lax.broadcasted_iota(jnp.int32, (rows, rows), 1) // patches
    keep = row_band >= key_band

    keep2 = jnp.concatenate([keep, jnp.full((rows, rows), True)], axis=1)

    def attend_local(h):
        at = lanes(h)

        @pl.when(c == 0)
        def _():
            loc_o[h], loc_s[h] = softmax_block(q_v[:, at], k_v[:, at], v_v[:, at], keep)

        @pl.when(c == 1)
        def _():
            loc_o[h], loc_s[h] = softmax_block(
                q_v[:, at],
                jnp.concatenate([k_v[:, at], sib_k[:, at]], axis=0),
                jnp.concatenate([v_v[:, at], sib_v[:, at]], axis=0),
                keep2,
            )

    def block(q_slot, h, key_at, key_count):
        q = qall[h, span(q_slot * 2 * rows, 2), :]
        o, s = softmax_block(q, kall[h, key_at : key_at + key_count, :] if isinstance(key_at, int)
                             else kall[h, pl.ds(pl.multiple_of(key_at, rows), key_count), :],
                             vall[h, key_at : key_at + key_count, :] if isinstance(key_at, int)
                             else vall[h, pl.ds(pl.multiple_of(key_at, rows), key_count), :])
        return o.astype(jnp.bfloat16), s.T[0:1, :]

    def deliver(q_slot, h, slot, chip, cc, do):
        for n, (src, dst) in enumerate(((out_p, part), (out_s, stat))):
            do(remote(src.at[q_slot, cc, h], dst.at[slot, c * half + h],
                      part_send.at[q_slot, cc, h, n], part_recv.at[slot, c * half + h, n], chip * 2 + cc))

    def compute(q_slot, h, key_at, key_count, slot, chip):
        keys = pl.ds(key_at, key_count)
        for cc in range(2):
            o, s = softmax_block(
                qall[h, span((q_slot * 2 + cc) * rows), :], kall[h, keys, :], vall[h, keys, :]
            )
            out_p[q_slot, cc, h] = o.astype(jnp.bfloat16)
            out_s[q_slot, cc, h] = s.T[0:1, :]
            deliver(q_slot, h, slot, chip, cc, start)

    def wait_local_kv(h):
        for n in range(2):
            own[h][n].wait()
        for n, dst in enumerate((kall, vall)):
            ref = dst.at[h, span(base + other * rows)]
            remote(ref, ref, sibh_send.at[h, n], sibh_recv.at[h, n], sib).wait_recv()

    def wait_own_q(h):
        own[h][2].wait()
        ref = qall.at[h, span((mid * 2 + other) * rows)]
        remote(ref, ref, sibh_send.at[h, 2], sibh_recv.at[h, 2], sib).wait_recv()

    def wait_q(j, h):
        for cc in range(2):
            ref = qall.at[h, span(((j - mid) * 2 + cc) * rows)]
            remote(ref, ref, q_send.at[0, cc, h], q_recv.at[j - mid, cc, h], sib).wait_recv()

    def wait_kv(i, h):
        for cc in range(2):
            for n, dst in enumerate((kall, vall)):
                ref = dst.at[h, span((i * 2 + cc) * rows)]
                remote(ref, ref, kv_send.at[0, cc, h, n], kv_recv.at[i, cc, h, n], sib).wait_recv()

    for item in range(heads):
        h = item // 2
        if item + WINDOW < heads:
            push(item, wait_send)
            push(item + WINDOW, start)
        if item % 2 == 0:
            wait_local_kv(h)
            wait_own_q(h)

            @pl.when(lower)
            def _():
                each(0, z, lambda i: wait_kv(i, h))

                @pl.when(z == hub)
                def _():
                    def body(n):
                        j = chips - 1 - n
                        wait_q(j, h)
                        compute(j - mid, h, 0, 2 * mid * rows, 0, j)
                    each(0, chips - mid, body)

                def body(i):
                    o, s = block(mid, h, i * 2 * rows, 2 * rows)
                    for cc in range(2):
                        @pl.when(cc == c)
                        def _():
                            part[i, c * half + h] = o[cc * rows : (cc + 1) * rows]
                            stat[i, c * half + h] = s[:, cc * rows : (cc + 1) * rows]

                        @pl.when(cc != c)
                        def _():
                            out_p[mid + i, cc, h] = o[cc * rows : (cc + 1) * rows]
                            out_s[mid + i, cc, h] = s[:, cc * rows : (cc + 1) * rows]
                            deliver(mid + i, h, i, z, cc, start)
                each(0, z, body)

        if item == 0:
            @pl.when(c == 1)
            def _():
                for n, dst in enumerate((sib_k, sib_v)):
                    remote(dst, dst, sib_send.at[n], sib_recv.at[n], sib).wait_recv()
        attend_local(item)
        if item % 2 == 1:
            @pl.when(jnp.logical_not(lower))
            def _():
                def body(j):
                    wait_q(j, h)
                    compute(j - mid, h, 0, 2 * rows, 1 + z - mid, j)
                each(z + 1, chips, body)

    def out_copy(head):
        at = lanes(head)
        return pltpu.make_async_copy(o_v.at[:, at], o_hbm.at[:, at], out_sem.at[head])

    def finish(head, from_me):
        at = lanes(head)

        def merge(slot, carry):
            acc, weight, top = carry
            @pl.when(jnp.logical_not(jnp.logical_and(lower, from_me)))
            def _():
                for n, dst in enumerate((part, stat)):
                    ref = dst.at[slot, head]
                    remote(ref, ref, part_send.at[0, 0, 0, n], part_recv.at[slot, head, n], sib).wait_recv()
            s = jnp.broadcast_to(stat[slot, head], (HDIM, rows)).T
            new_top = jnp.maximum(top, s)
            a, b = jnp.exp2(top - new_top), jnp.exp2(s - new_top)
            return acc * a + part[slot, head].astype(jnp.float32) * b, weight * a + b, new_top

        acc, weight, _ = lax.fori_loop(
            0, jnp.where(lower, z, z - mid + 1), merge,
            (loc_o[head], jnp.ones((rows, HDIM), jnp.float32), loc_s[head]),
        )
        o_v[:, at] = (acc / weight).astype(o_v.dtype)
        out_copy(head).start()

    for h in range(half):
        for cc in range(2):
            finish(cc * half + h, cc == c)

    for item in range(max(heads - WINDOW, 0), heads):
        push(item, wait_send)
    for head in range(heads):
        out_copy(head).wait()
    for h in range(half):
        sib_push(h, wait_send)

        @pl.when(z == hub)
        def _():
            def body(j):
                for cc in range(2):
                    deliver(j - mid, h, 0, j, cc, wait_send)
            each(mid, chips, body)

        @pl.when(lower)
        def _():
            each(0, z, lambda i: deliver(mid + i, h, i, z, other, wait_send))

        @pl.when(jnp.logical_not(lower))
        def _():
            def body(j):
                for cc in range(2):
                    deliver(j - mid, h, 1 + z - mid, j, cc, wait_send)
            each(z + 1, chips, body)
    sib_whole(wait_send)


def shards(chips, queries, keys, values):
    band_count, patch_count, width = queries.shape
    rows = band_count * patch_count
    heads = width // HDIM
    half = heads // 2
    mid = chips // 2
    bf16, f32 = jnp.bfloat16, jnp.float32
    dma = pltpu.SemaphoreType.DMA
    out = pl.pallas_call(
        functools.partial(kernel, chips, patch_count),
        out_shape=jax.ShapeDtypeStruct((rows, width), bf16),
        in_specs=[pl.BlockSpec(memory_space=pl.ANY)] * 3,
        out_specs=pl.BlockSpec(memory_space=pl.ANY),
        scratch_shapes=[
            pltpu.VMEM((rows, width), bf16),
            pltpu.VMEM((rows, width), bf16),
            pltpu.VMEM((rows, width), bf16),
            pltpu.VMEM((rows, width), bf16),
            pltpu.VMEM((rows, width), bf16),
            pltpu.VMEM((rows, width), bf16),
            pltpu.VMEM((half, 2 * mid * rows, HDIM), bf16),
            pltpu.VMEM((half, 2 * mid * rows, HDIM), bf16),
            pltpu.VMEM((half, 2 * (mid + 1) * rows, HDIM), bf16),
            pltpu.VMEM((2 * mid, 2, half, rows, HDIM), bf16),
            pltpu.VMEM((2 * mid, 2, half, 1, rows), f32),
            pltpu.VMEM((mid, heads, rows, HDIM), bf16),
            pltpu.VMEM((mid, heads, 1, rows), f32),
            pltpu.VMEM((heads, rows, HDIM), f32),
            pltpu.VMEM((heads, rows, HDIM), f32),
            dma((3,)),
            dma((half, 3)),
            dma((mid, 2, half, 2)),
            dma((mid, 2, half, 2)),
            dma((mid, 2, half)),
            dma((mid, 2, half)),
            dma((2,)),
            dma((2,)),
            dma((half, 3)),
            dma((half, 3)),
            dma((2 * mid, 2, half, 2)),
            dma((mid, heads, 2)),
            dma((heads,)),
        ],
        compiler_params=pltpu.CompilerParams(
            collective_id=0, has_side_effects=True, vmem_limit_bytes=62 * 1024 * 1024
        ),
        cost_estimate=pl.CostEstimate(
            flops=4 * rows * chips * rows * width, bytes_accessed=8 * rows * width, transcendentals=0
        ),
    )(*(a.reshape(rows, width) for a in (queries, keys, values)))
    return out.reshape(band_count, patch_count, width)


def solution(mesh):
    spec = P(("dp", "blk"), None, None)
    return jax.shard_map(
        functools.partial(shards, mesh.shape["blk"] // 2),
        mesh=mesh,
        in_specs=(spec, spec, spec),
        out_specs=spec,
        check_vma=False,
    )
```

```python
import functools
import math

import jax
import jax.numpy as jnp
from jax import lax
from jax.experimental import pallas as pl
from jax.experimental.pallas import tpu as pltpu
from jax.sharding import PartitionSpec as P

HDIM = 128
MESH = pl.DeviceIdType.MESH
WINDOW = 3
SCALE = HDIM ** (-0.5) * math.log2(math.e)


def softmax_block(q, k, v, keep=None):
    s = lax.dot_general(q, k, (((1,), (1,)), ((), ())), preferred_element_type=jnp.float32)
    if keep is not None:
        s = jnp.where(keep, s, jnp.float32(-1e30))
    top = jnp.max(s, axis=1, keepdims=True)
    p = jnp.exp2((s - top) * SCALE)
    p = p.astype(jnp.bfloat16)
    ve = jnp.concatenate([v, jnp.ones_like(v)], axis=1)
    o = jnp.dot(p, ve, preferred_element_type=jnp.float32)
    total = o[:, HDIM:]
    return o[:, :HDIM] / total, top * SCALE + jnp.log2(total)


def kernel(
    chips, patches,
    q_hbm, k_hbm, v_hbm, o_hbm,
    o_v, q_v, k_v, v_v, sib_k, sib_v, kall, vall, qall, out_p, out_s, part, stat, loc_o, loc_s,
    load_sem, own_sem, kv_send, kv_recv, q_send, q_recv, sib_send, sib_recv, sibh_send, sibh_recv,
    part_send, part_recv, out_sem,
):
    rows, width = q_v.shape
    heads = width // HDIM
    half = heads // 2
    mid = chips // 2
    hub = mid - 1
    upper = chips - mid
    group = 2 if upper % 2 == 0 else 1
    me = lax.axis_index("blk")
    z, c = me // 2, me % 2
    other = 1 - c
    sib = z * 2 + other
    lower = z < mid
    base = jnp.where(lower, z * (2 * rows), 0)

    def remote(src, dst, send, recv, dev):
        return pltpu.make_async_remote_copy(
            src_ref=src, dst_ref=dst, send_sem=send, recv_sem=recv,
            device_id={"blk": dev}, device_id_type=MESH,
        )

    def lanes(h):
        return pl.ds(pl.multiple_of(h * HDIM, HDIM), HDIM)

    def span(at, count=1):
        return pl.ds(pl.multiple_of(at, rows), count * rows)

    def each(lo, hi, body):
        def step(i, carry):
            body(i)
            return carry
        lax.fori_loop(lo, hi, step, 0)

    loads = [
        pltpu.make_async_copy(src, dst, load_sem.at[n])
        for n, (src, dst) in enumerate(((q_hbm, q_v), (k_hbm, k_v), (v_hbm, v_v)))
    ]
    for copy in loads:
        copy.start()
    own = []
    for h in range(half):
        at = lanes(c * half + h)
        own.append((
            pltpu.make_async_copy(k_hbm.at[:, at], kall.at[h, span(base + c * rows)], own_sem.at[h, 0]),
            pltpu.make_async_copy(v_hbm.at[:, at], vall.at[h, span(base + c * rows)], own_sem.at[h, 1]),
            pltpu.make_async_copy(q_hbm.at[:, at], qall.at[h, span((mid * 2 + c) * rows)], own_sem.at[h, 2]),
        ))
        for copy in own[-1]:
            copy.start()

    barrier = pltpu.get_barrier_semaphore()
    count = 2 * chips
    for step in range(1, count):
        dev = lax.rem(me + step, count)
        y = dev // 2

        @pl.when((lower & (y < mid)) | ((z >= mid) & (y >= mid)) | (z == hub) | (y == hub))
        def _():
            pl.semaphore_signal(barrier, inc=1, device_id={"blk": dev}, device_id_type=MESH)
    pl.semaphore_wait(barrier, jnp.where(
        z == hub, count - 1, jnp.where(lower, 2 * mid - 1, 2 * (chips - mid) + 1)
    ))

    def kv_push(h, cc, do):
        def to(j):
            at = lanes(cc * half + h)
            for n, (src, dst) in enumerate(((k_hbm, kall), (v_hbm, vall))):
                do(remote(src.at[:, at], dst.at[h, span((z * 2 + c) * rows)],
                          kv_send.at[j, cc, h, n], kv_recv.at[z, c, h, n], j * 2 + cc))
        each(z + 1, jnp.where(lower, mid, 0), to)

    def q_push(h, cc, do):
        def to(i):
            do(remote(q_hbm.at[:, lanes(cc * half + h)], qall.at[h, span(((z - mid) * 2 + c) * rows)],
                      q_send.at[i - hub, cc, h], q_recv.at[z - mid, c, h], i * 2 + cc))
        each(hub, jnp.where(lower, 0, z), to)

    def push(item, do):
        h, cc = item // 2, item % 2
        kv_push(h, cc, do)
        q_push(h, cc, do)

    def sib_push(h, do):
        at = lanes(other * half + h)
        for n, (src, dst, row) in enumerate((
            (k_v, kall, base + c * rows), (v_v, vall, base + c * rows), (q_v, qall, (mid * 2 + c) * rows),
        )):
            do(remote(src.at[:, at], dst.at[h, span(row)], sibh_send.at[h, n], sibh_recv.at[h, n], sib))

    def sib_whole(do):
        @pl.when(c == 0)
        def _():
            for n, (src, dst) in enumerate(((k_v, sib_k), (v_v, sib_v))):
                do(remote(src, dst, sib_send.at[n], sib_recv.at[n], sib))

    def start(copy):
        copy.start()

    def wait_send(copy):
        copy.wait_send()

    for item in range(min(WINDOW, heads)):
        push(item, start)
    for copy in loads:
        copy.wait()
    for h in range(half):
        sib_push(h, start)
    sib_whole(start)

    row_band = lax.broadcasted_iota(jnp.int32, (rows, rows), 0) // patches
    key_band = lax.broadcasted_iota(jnp.int32, (rows, rows), 1) // patches
    keep = row_band >= key_band

    keep2 = jnp.concatenate([keep, jnp.full((rows, rows), True)], axis=1)

    def attend_local(h):
        at = lanes(h)

        @pl.when(c == 0)
        def _():
            loc_o[h], loc_s[h] = softmax_block(q_v[:, at], k_v[:, at], v_v[:, at], keep)

        @pl.when(c == 1)
        def _():
            loc_o[h], loc_s[h] = softmax_block(
                q_v[:, at],
                jnp.concatenate([k_v[:, at], sib_k[:, at]], axis=0),
                jnp.concatenate([v_v[:, at], sib_v[:, at]], axis=0),
                keep2,
            )

    def block(q_slot, h, key_at, key_count):
        q = qall[h, span(q_slot * 2 * rows, 2), :]
        o, s = softmax_block(q, kall[h, key_at : key_at + key_count, :] if isinstance(key_at, int)
                             else kall[h, pl.ds(pl.multiple_of(key_at, rows), key_count), :],
                             vall[h, key_at : key_at + key_count, :] if isinstance(key_at, int)
                             else vall[h, pl.ds(pl.multiple_of(key_at, rows), key_count), :])
        return o.astype(jnp.bfloat16), s.T[0:1, :]

    def deliver(q_slot, h, slot, chip, cc, do):
        for n, (src, dst) in enumerate(((out_p, part), (out_s, stat))):
            do(remote(src.at[q_slot, cc, h], dst.at[slot, c * half + h],
                      part_send.at[q_slot, cc, h, n], part_recv.at[slot, c * half + h, n], chip * 2 + cc))

    def compute(q_slot, h, key_at, key_count, slot, chip):
        o, s = block(q_slot, h, key_at, key_count)
        for cc in range(2):
            out_p[q_slot, cc, h] = o[cc * rows : (cc + 1) * rows]
            out_s[q_slot, cc, h] = s[:, cc * rows : (cc + 1) * rows]
            deliver(q_slot, h, slot, chip, cc, start)

    def wait_local_kv(h):
        for n in range(2):
            own[h][n].wait()
        for n, dst in enumerate((kall, vall)):
            ref = dst.at[h, span(base + other * rows)]
            remote(ref, ref, sibh_send.at[h, n], sibh_recv.at[h, n], sib).wait_recv()

    def wait_own_q(h):
        own[h][2].wait()
        ref = qall.at[h, span((mid * 2 + other) * rows)]
        remote(ref, ref, sibh_send.at[h, 2], sibh_recv.at[h, 2], sib).wait_recv()

    def wait_q(j, h):
        for cc in range(2):
            ref = qall.at[h, span(((j - mid) * 2 + cc) * rows)]
            remote(ref, ref, q_send.at[0, cc, h], q_recv.at[j - mid, cc, h], sib).wait_recv()

    def wait_kv(i, h):
        for cc in range(2):
            for n, dst in enumerate((kall, vall)):
                ref = dst.at[h, span((i * 2 + cc) * rows)]
                remote(ref, ref, kv_send.at[0, cc, h, n], kv_recv.at[i, cc, h, n], sib).wait_recv()

    for item in range(heads):
        h = item // 2
        if item + WINDOW < heads:
            push(item, wait_send)
            push(item + WINDOW, start)
        if item % 2 == 0:
            wait_local_kv(h)
            wait_own_q(h)

            @pl.when(lower)
            def _():
                each(0, z, lambda i: wait_kv(i, h))

                @pl.when(z == hub)
                def _():
                    def body(n):
                        first = (upper // group - 1 - n) * group
                        for g in range(group):
                            wait_q(mid + first + g, h)
                        keys = 2 * mid * rows
                        o, s = softmax_block(
                            qall[h, span(first * 2 * rows, 2 * group), :], kall[h, 0:keys, :], vall[h, 0:keys, :]
                        )
                        o, s = o.astype(jnp.bfloat16), s.T[0:1, :]
                        for g in reversed(range(group)):
                            for cc in range(2):
                                at = (g * 2 + cc) * rows
                                out_p[first + g, cc, h] = o[at : at + rows]
                                out_s[first + g, cc, h] = s[:, at : at + rows]
                                deliver(first + g, h, 0, mid + first + g, cc, start)
                    each(0, upper // group, body)

                def body(i):
                    o, s = block(mid, h, i * 2 * rows, 2 * rows)
                    for cc in range(2):
                        @pl.when(cc == c)
                        def _():
                            part[i, c * half + h] = o[cc * rows : (cc + 1) * rows]
                            stat[i, c * half + h] = s[:, cc * rows : (cc + 1) * rows]

                        @pl.when(cc != c)
                        def _():
                            out_p[mid + i, cc, h] = o[cc * rows : (cc + 1) * rows]
                            out_s[mid + i, cc, h] = s[:, cc * rows : (cc + 1) * rows]
                            deliver(mid + i, h, i, z, cc, start)
                each(0, z, body)

        if item == 0:
            @pl.when(c == 1)
            def _():
                for n, dst in enumerate((sib_k, sib_v)):
                    remote(dst, dst, sib_send.at[n], sib_recv.at[n], sib).wait_recv()
        attend_local(item)
        if item % 2 == 1:
            @pl.when(jnp.logical_not(lower))
            def _():
                def body(j):
                    wait_q(j, h)
                    compute(j - mid, h, 0, 2 * rows, 1 + z - mid, j)
                each(z + 1, chips, body)

    def out_copy(head):
        at = lanes(head)
        return pltpu.make_async_copy(o_v.at[:, at], o_hbm.at[:, at], out_sem.at[head])

    def finish(head, from_me):
        at = lanes(head)

        def merge(slot, carry):
            acc, weight, top = carry
            @pl.when(jnp.logical_not(jnp.logical_and(lower, from_me)))
            def _():
                for n, dst in enumerate((part, stat)):
                    ref = dst.at[slot, head]
                    remote(ref, ref, part_send.at[0, 0, 0, n], part_recv.at[slot, head, n], sib).wait_recv()
            s = jnp.broadcast_to(stat[slot, head], (HDIM, rows)).T
            new_top = jnp.maximum(top, s)
            a, b = jnp.exp2(top - new_top), jnp.exp2(s - new_top)
            return acc * a + part[slot, head].astype(jnp.float32) * b, weight * a + b, new_top

        acc, weight, _ = lax.fori_loop(
            0, jnp.where(lower, z, z - mid + 1), merge,
            (loc_o[head], jnp.ones((rows, HDIM), jnp.float32), loc_s[head]),
        )
        o_v[:, at] = (acc / weight).astype(o_v.dtype)
        out_copy(head).start()

    for h in range(half):
        for cc in range(2):
            finish(cc * half + h, cc == c)

    for item in range(max(heads - WINDOW, 0), heads):
        push(item, wait_send)
    for head in range(heads):
        out_copy(head).wait()
    for h in range(half):
        sib_push(h, wait_send)

        @pl.when(z == hub)
        def _():
            def body(j):
                for cc in range(2):
                    deliver(j - mid, h, 0, j, cc, wait_send)
            each(mid, chips, body)

        @pl.when(lower)
        def _():
            each(0, z, lambda i: deliver(mid + i, h, i, z, other, wait_send))

        @pl.when(jnp.logical_not(lower))
        def _():
            def body(j):
                for cc in range(2):
                    deliver(j - mid, h, 1 + z - mid, j, cc, wait_send)
            each(z + 1, chips, body)
    sib_whole(wait_send)


def shards(chips, queries, keys, values):
    band_count, patch_count, width = queries.shape
    rows = band_count * patch_count
    heads = width // HDIM
    half = heads // 2
    mid = chips // 2
    bf16, f32 = jnp.bfloat16, jnp.float32
    dma = pltpu.SemaphoreType.DMA
    out = pl.pallas_call(
        functools.partial(kernel, chips, patch_count),
        out_shape=jax.ShapeDtypeStruct((rows, width), bf16),
        in_specs=[pl.BlockSpec(memory_space=pl.ANY)] * 3,
        out_specs=pl.BlockSpec(memory_space=pl.ANY),
        scratch_shapes=[
            pltpu.VMEM((rows, width), bf16),
            pltpu.VMEM((rows, width), bf16),
            pltpu.VMEM((rows, width), bf16),
            pltpu.VMEM((rows, width), bf16),
            pltpu.VMEM((rows, width), bf16),
            pltpu.VMEM((rows, width), bf16),
            pltpu.VMEM((half, 2 * mid * rows, HDIM), bf16),
            pltpu.VMEM((half, 2 * mid * rows, HDIM), bf16),
            pltpu.VMEM((half, 2 * (mid + 1) * rows, HDIM), bf16),
            pltpu.VMEM((2 * mid, 2, half, rows, HDIM), bf16),
            pltpu.VMEM((2 * mid, 2, half, 1, rows), f32),
            pltpu.VMEM((mid, heads, rows, HDIM), bf16),
            pltpu.VMEM((mid, heads, 1, rows), f32),
            pltpu.VMEM((heads, rows, HDIM), f32),
            pltpu.VMEM((heads, rows, HDIM), f32),
            dma((3,)),
            dma((half, 3)),
            dma((mid, 2, half, 2)),
            dma((mid, 2, half, 2)),
            dma((mid, 2, half)),
            dma((mid, 2, half)),
            dma((2,)),
            dma((2,)),
            dma((half, 3)),
            dma((half, 3)),
            dma((2 * mid, 2, half, 2)),
            dma((mid, heads, 2)),
            dma((heads,)),
        ],
        compiler_params=pltpu.CompilerParams(
            collective_id=0, has_side_effects=True, vmem_limit_bytes=62 * 1024 * 1024
        ),
        cost_estimate=pl.CostEstimate(
            flops=4 * rows * chips * rows * width, bytes_accessed=8 * rows * width, transcendentals=0
        ),
    )(*(a.reshape(rows, width) for a in (queries, keys, values)))
    return out.reshape(band_count, patch_count, width)


def solution(mesh):
    spec = P(("dp", "blk"), None, None)
    return jax.shard_map(
        functools.partial(shards, mesh.shape["blk"] // 2),
        mesh=mesh,
        in_specs=(spec, spec, spec),
        out_specs=spec,
        check_vma=False,
    )
```
